32 devices in a mesh: dop: 4 (over y, core), rng: 8 (over z, x).
Axes of the slice: x: 2, y: 2, z: 4, core: 2. Of those that a mesh axis runs over, the one named last changes fastest.
Arguments:
- echoes: bfloat16 [2048, 2, 32, 128], P(('rng', 'dop')), may hold values from -60 to 60
- training: int32 [128, 2048], P('dop', 'rng'), may hold values 0 or 1
- look_index: int32 [64], replicated, may hold values from 0 to 255
Outputs:
- beam_output: float32 [128, 2, 64, 2048], P('dop', None, None, 'rng')
The draws below stay inside these ranges and needn't reach their ends.
All inputs are finite; a program needn't handle non-finite values. No bound on the sum of `training` on one device may be relied on, other than what follows from the above.
Results may differ from the reference program's by a relative error of at most 0.012.
The reference program's roundings to bfloat16 on the way (of `twiddle`, `spectra`, `snapshot` and `weights`) count: a program that leaves them out, or rounds other values in their place, can miss the bound.
Values may be sent and summed in bfloat16 or wider, within the bound.
A program may use at most 128 MiB of HBM per device.

```python
import math
import jax
import jax.numpy as jnp
from jax import lax

CH = 32
PULSES = 128
LOOKS = 64
ANGLES = 256
DOPPLER = 128
RANGE = 2048
RANGE_DEV = 256
SNAP = 192


def draw_echoes(key, part):
    key_list = jax.random.split(key, 9)
    cell_ids = jnp.arange(RANGE).astype(jnp.float32)
    channel_ids = jnp.arange(CH).astype(jnp.float32)
    pulse_ids = jnp.arange(PULSES).astype(jnp.float32)
    range_trend = jnp.exp((1.0 - cell_ids / RANGE) * math.log(3.0))
    roughness = jnp.exp(jax.random.uniform(key_list[0], (RANGE,), jnp.float32, math.log(0.5), math.log(2.0)))
    amplitude = 0.5 * range_trend * roughness
    channel_gain = jnp.exp(jax.random.uniform(key_list[1], (CH,), jnp.float32, math.log(0.55), math.log(1.8)))
    noise_draw = jax.random.normal(key_list[2], (RANGE, 2, CH, PULSES), jnp.float32)
    clutter_low = 0.8
    clutter_high = 2.0
    real_sum = amplitude[:, None, None] * noise_draw[:, 0]
    imag_sum = amplitude[:, None, None] * noise_draw[:, 1]
    jammer_count = 12
    jammer_sines = -0.95 + 1.9 * (jnp.arange(jammer_count).astype(jnp.float32) + jax.random.uniform(key_list[3], (jammer_count,), jnp.float32, 0.2, 0.8)) / jammer_count
    jammer_levels = jnp.exp(jax.random.uniform(key_list[4], (jammer_count,), jnp.float32, math.log(0.5), math.log(5.0)))
    jammer_signal = jax.random.normal(key_list[5], (jammer_count, 2, RANGE, PULSES), jnp.float32)
    for jammer_id in range(jammer_count):
        phases = jnp.pi * channel_ids * jammer_sines[jammer_id]
        cos_phase = jnp.cos(phases)[None, :, None]
        sin_phase = jnp.sin(phases)[None, :, None]
        signal_real = jammer_signal[jammer_id, 0][:, None, :]
        signal_imag = jammer_signal[jammer_id, 1][:, None, :]
        real_sum = real_sum + jammer_levels[jammer_id] * (cos_phase * signal_real - sin_phase * signal_imag)
        imag_sum = imag_sum + jammer_levels[jammer_id] * (sin_phase * signal_real + cos_phase * signal_imag)
    patch_count = 4
    clutter_sines = jax.random.uniform(key_list[6], (RANGE, patch_count), jnp.float32, -1.0, 1.0)
    clutter_levels = amplitude[:, None] * jnp.exp(jax.random.uniform(key_list[7], (RANGE, patch_count), jnp.float32, math.log(clutter_low), math.log(clutter_high)))
    clutter_amps = jax.random.normal(key_list[8], (RANGE, patch_count, 2), jnp.float32)
    for patch_id in range(patch_count):
        sine_col = clutter_sines[:, patch_id][:, None, None]
        phase_grid = jnp.pi * channel_ids[None, :, None] * sine_col + 2.0 * jnp.pi * 0.49 * sine_col * pulse_ids[None, None, :]
        amp_real = (clutter_levels[:, patch_id] * clutter_amps[:, patch_id, 0])[:, None, None]
        amp_imag = (clutter_levels[:, patch_id] * clutter_amps[:, patch_id, 1])[:, None, None]
        cos_grid = jnp.cos(phase_grid)
        sin_grid = jnp.sin(phase_grid)
        real_sum = real_sum + amp_real * cos_grid - amp_imag * sin_grid
        imag_sum = imag_sum + amp_real * sin_grid + amp_imag * cos_grid
    values = jnp.stack([real_sum, imag_sum], axis=1) * channel_gain[None, None, :, None]
    return jnp.clip(values, -60.0, 60.0).astype(jnp.bfloat16)


def place_ends(values, stream_key, least, top_value):
    extent = values.shape
    index_at = [jax.random.randint(jax.random.fold_in(stream_key, axis), (), 0, extent[axis]) for axis in range(len(extent))]
    values = values.at[tuple(index_at)].set(least)
    longest = extent.index(max(extent))
    index_at[longest] = (index_at[longest] + 1) % extent[longest]
    return values.at[tuple(index_at)].set(top_value)


def setup_inputs(seed: int = 0) -> dict:
    streams_of = jax.random.split(jax.random.key(seed), 4)
    echoes = draw_echoes(jax.random.fold_in(streams_of[3], 71), 0)
    training = place_ends((jax.random.randint(streams_of[1], (DOPPLER, RANGE), 0, 4) < 3).astype(jnp.int32), jax.random.fold_in(streams_of[1], 1), 0, 1)
    look_index = place_ends(jax.random.randint(streams_of[2], (LOOKS,), 0, ANGLES), jax.random.fold_in(streams_of[2], 1), 0, ANGLES - 1).astype(jnp.int32)
    return {"echoes": echoes, "training": training, "look_index": look_index}


loading = 0.1
epsilon = 1e-06
highest = lax.Precision.HIGHEST

def twiddles():
    pulse_ids = jnp.arange(PULSES, dtype=jnp.int32)
    phase_ids = pulse_ids[:, None] * pulse_ids[None, :] % PULSES
    angles = phase_ids.astype(jnp.float32) * (2.0 * jnp.pi / PULSES)
    return jnp.concatenate([jnp.cos(angles), jnp.sin(angles)], axis=0).astype(jnp.bfloat16)

def doppler_block(echo_rows, twiddle):
    product = jnp.einsum('kp,rqcp->krqc', twiddle.astype(jnp.float32), echo_rows.astype(jnp.float32), precision=highest)
    cosine = product[:PULSES]
    sine = product[PULSES:]
    real_part = cosine[:, :, 0] + sine[:, :, 1]
    imag_part = cosine[:, :, 1] - sine[:, :, 0]
    return jnp.stack([real_part, imag_part], axis=2).reshape(PULSES, echo_rows.shape[0], 2 * CH).astype(jnp.bfloat16)

def steering(look_index):
    sines = -1.0 + (2.0 * look_index.astype(jnp.float32) + 1.0) / ANGLES
    channel_ids = jnp.arange(CH).astype(jnp.float32)
    phases = jnp.pi * channel_ids[:, None] * sines[None, :]
    zeros = jnp.zeros((CH, LOOKS), jnp.float32)
    return jnp.stack([zeros, zeros, jnp.cos(phases), jnp.sin(phases), zeros, zeros]).reshape(SNAP, LOOKS)

def full_matrix(gram_matrix):
    gram_grid = gram_matrix.reshape(3, 2, CH, 3, 2, CH)
    flipped = gram_grid[:, ::-1, :, :, ::-1, :]
    flip_sign = jnp.array([1.0, -1.0], jnp.float32)
    sign_grid = (flip_sign[:, None] * flip_sign[None, :]).reshape(1, 2, 1, 1, 2, 1)
    return (gram_grid + sign_grid * flipped).reshape(SNAP, SNAP)

def mvdr_weights(matrix, steer):
    bin_count = matrix.shape[0]
    power = jnp.trace(matrix, axis1=1, axis2=2) / SNAP + epsilon
    regular = matrix / power[:, None, None] + loading * jnp.eye(SNAP, dtype=jnp.float32)
    factor = jnp.linalg.cholesky(regular)
    targets = jnp.broadcast_to(steer, (bin_count, SNAP, LOOKS))
    forward = lax.linalg.triangular_solve(factor, targets, left_side=True, lower=True)
    solved = lax.linalg.triangular_solve(factor, forward, left_side=True, lower=True, transpose_a=True)
    gains = lax.optimization_barrier(jnp.sum(targets * solved, axis=1))
    unit = solved / jnp.sqrt(gains)[:, None, :]
    shaped = unit.reshape(bin_count, 3, 2, CH, LOOKS)
    rotated = jnp.stack([-shaped[:, :, 1], shaped[:, :, 0]], axis=2)
    return jnp.concatenate([unit, rotated.reshape(bin_count, SNAP, LOOKS)], axis=2).astype(jnp.bfloat16)

def reference(echoes, training, look_index):
    twiddle = twiddles()
    range_blocks = echoes.reshape(RANGE // RANGE_DEV, RANGE_DEV, 2, CH, PULSES)
    spectra_blocks = lax.map(lambda rows: doppler_block(rows, twiddle), range_blocks)
    spectra = jnp.transpose(spectra_blocks, (1, 0, 2, 3)).reshape(DOPPLER, RANGE, 2 * CH)
    steer = steering(look_index)

    def one_bin(bin_id):
        neighbours = ((bin_id + jnp.arange(3, dtype=jnp.int32) - 1 + DOPPLER) % DOPPLER).astype(jnp.int32)
        picked = jnp.take(spectra, neighbours, axis=0)
        snapshot = jnp.transpose(picked, (1, 0, 2)).reshape(RANGE, SNAP).astype(jnp.float32)
        weight_row = lax.dynamic_index_in_dim(training, bin_id, 0, keepdims=False).astype(jnp.float32)
        gram_matrix = jnp.dot((snapshot * weight_row[:, None]).T, snapshot, precision=highest)
        matrix = full_matrix(gram_matrix)
        weights = mvdr_weights(matrix[None], steer)[0]
        output = jnp.dot(weights.astype(jnp.float32).T, snapshot.T, precision=highest)
        return output.reshape(2, LOOKS, RANGE)
    return lax.map(one_bin, jnp.arange(DOPPLER, dtype=jnp.int32))
```

```python
import functools

import jax
import jax.numpy as jnp
import numpy as np
from jax import lax
from jax.experimental import pallas as pl
from jax.experimental.pallas import tpu as pltpu
from jax.sharding import PartitionSpec as P

CH = 32
PULSES = 128
LOOKS = 64
ANGLES = 256

loading = 0.1
epsilon = 1e-06
highest = lax.Precision.HIGHEST
MESH = pl.DeviceIdType.MESH
bf16 = jnp.bfloat16
f32 = jnp.float32


def twiddle_table():
    pulse_ids = np.arange(PULSES)
    bins = np.arange(-1, PULSES + 1) % PULSES
    angles = ((bins[:, None] * pulse_ids[None, :]) % PULSES).astype(np.float32) * np.float32(
        2.0 * np.pi / PULSES
    )
    cosine, sine = np.cos(angles), np.sin(angles)
    table = np.stack([np.stack([cosine, sine], 1), np.stack([-sine, cosine], 1)], 0)
    return jnp.asarray(table, bf16)


def steering(look_index):
    sines = -1.0 + (2.0 * look_index.astype(f32) + 1.0) / ANGLES
    channel_ids = jnp.arange(CH).astype(f32)
    phases = jnp.pi * channel_ids[:, None] * sines[None, :]
    return jnp.concatenate([jnp.cos(phases), jnp.sin(phases)], axis=0)


def exchange_kernel(D, R, spec, mask, wide, mine, masks, send_m, recv_m, send_x, recv_x,
                    send_w, recv_w, own):
    N = D * R
    bins = PULSES // D
    share = bins // R
    d, g = lax.axis_index("dop"), lax.axis_index("rng")
    me = g * D + d
    barrier = pltpu.get_barrier_semaphore()

    def where(j):
        t = lax.rem(me + j, N)
        return t, lax.rem(t, D), t // D

    def greet(j, c):
        _, td, tg = where(j)
        pl.semaphore_signal(barrier, inc=1, device_id=(td, tg), device_id_type=MESH)
        return c

    lax.fori_loop(1, N, greet, 0)
    local = [
        pltpu.make_async_copy(mask.at[g], masks.at[g], own.at[0]),
        pltpu.make_async_copy(spec.at[pl.ds(d * bins + g * share, share + 2)], mine.at[me], own.at[1]),
        pltpu.make_async_copy(spec.at[pl.ds(d * bins, bins + 2)], wide.at[d], own.at[2]),
    ]
    for copy in local:
        copy.start()
    pl.semaphore_wait(barrier, N - 1)

    def mask_copy(j):
        tg = lax.rem(g + j, R)
        return pltpu.make_async_remote_copy(
            mask.at[tg], masks.at[g], send_m.at[j], recv_m.at[g], device_id=(d, tg),
            device_id_type=MESH)

    def mine_copy(j):
        _, td, tg = where(j)
        return pltpu.make_async_remote_copy(
            spec.at[pl.ds(td * bins + tg * share, share + 2)], mine.at[me], send_x.at[j],
            recv_x.at[me], device_id=(td, tg), device_id_type=MESH)

    def wide_copy(j):
        td = lax.rem(d + j, D)
        return pltpu.make_async_remote_copy(
            spec.at[pl.ds(td * bins, bins + 2)], wide.at[d], send_w.at[j], recv_w.at[d],
            device_id=(td, g), device_id_type=MESH)

    def start(make):
        def run(j, c):
            make(j).start()
            return c
        return run

    lax.fori_loop(1, R, start(mask_copy), 0)
    lax.fori_loop(1, N, start(mine_copy), 0)
    lax.fori_loop(1, D, start(wide_copy), 0)

    def end_mask(j, c):
        src = lax.rem(g + j, R)
        mask_copy(j).wait_send()
        pltpu.make_async_remote_copy(
            mask.at[0], masks.at[src], send_m.at[j], recv_m.at[src], device_id=(d, src),
            device_id_type=MESH).wait_recv()
        return c

    def end_mine(j, c):
        src, sd, sg = where(j)
        mine_copy(j).wait_send()
        pltpu.make_async_remote_copy(
            spec.at[pl.ds(0, share + 2)], mine.at[src], send_x.at[j], recv_x.at[src],
            device_id=(sd, sg), device_id_type=MESH).wait_recv()
        return c

    def end_wide(j, c):
        src = lax.rem(d + j, D)
        wide_copy(j).wait_send()
        pltpu.make_async_remote_copy(
            spec.at[pl.ds(0, bins + 2)], wide.at[src], send_w.at[j], recv_w.at[src],
            device_id=(src, g), device_id_type=MESH).wait_recv()
        return c

    lax.fori_loop(1, R, end_mask, 0)
    lax.fori_loop(1, N, end_mine, 0)
    lax.fori_loop(1, D, end_wide, 0)
    for copy in local:
        copy.wait()


def gather_kernel(R, unit, out, send, recv, own):
    d, g = lax.axis_index("dop"), lax.axis_index("rng")
    barrier = pltpu.get_barrier_semaphore()

    def greet(j, c):
        pl.semaphore_signal(barrier, inc=1, device_id=(d, lax.rem(g + j, R)), device_id_type=MESH)
        return c

    lax.fori_loop(1, R, greet, 0)
    local = pltpu.make_async_copy(unit, out.at[g], own)
    local.start()
    pl.semaphore_wait(barrier, R - 1)

    def make(j):
        tg = lax.rem(g + j, R)
        return pltpu.make_async_remote_copy(
            unit, out.at[g], send.at[j], recv.at[g], device_id=(d, tg), device_id_type=MESH)

    def begin(j, c):
        make(j).start()
        return c

    def end(j, c):
        src = lax.rem(g + j, R)
        make(j).wait_send()
        pltpu.make_async_remote_copy(
            unit, out.at[src], send.at[j], recv.at[src], device_id=(d, src),
            device_id_type=MESH).wait_recv()
        return c

    lax.fori_loop(1, R, begin, 0)
    lax.fori_loop(1, R, end, 0)
    local.wait()


def invert(re, im):
    width = re.shape[1]
    lane = lax.broadcasted_iota(jnp.int32, (CH, width), 1)
    row = lax.broadcasted_iota(jnp.int32, (CH, width), 0)
    base = lane // CH * CH
    col = lane - base
    for k in range(CH):
        pick = base + k
        cr = jnp.take_along_axis(re, pick, axis=1)
        ci = jnp.take_along_axis(im, pick, axis=1)
        at_col, at_row = col == k, row == k
        scale = 1.0 / cr[k:k + 1]
        rr = jnp.where(at_col[:1], 1.0, re[k:k + 1]) * scale
        ri = jnp.where(at_col[:1], 0.0, im[k:k + 1]) * scale
        clear = jnp.logical_or(at_col, at_row)
        cr = jnp.where(at_row, -1.0, cr)
        ci = jnp.where(at_row, 0.0, ci)
        re = jnp.where(clear, 0.0, re) - (cr * rr - ci * ri)
        im = jnp.where(clear, 0.0, im) - (cr * ri + ci * rr)
    return re, im


def stacked_form(re, im):
    return jnp.concatenate([re, im], axis=0)


def full_form(stacked):
    re, im = stacked[:CH], stacked[CH:]
    return jnp.concatenate(
        [jnp.concatenate([re, -im], axis=1), jnp.concatenate([im, re], axis=1)], axis=0)


def mul(a, b):
    return jnp.dot(a, b, precision=highest, preferred_element_type=f32)


def invert_all(blocks):
    lanes = 128 // CH
    packed = (blocks * lanes)[:lanes] if len(blocks) < lanes else blocks
    re, im = invert(
        jnp.concatenate([block[:CH] for block in packed], axis=1),
        jnp.concatenate([block[CH:] for block in packed], axis=1))
    return [
        stacked_form(re[:, i * CH:(i + 1) * CH], im[:, i * CH:(i + 1) * CH])
        for i in range(len(blocks))
    ]


def weights_kernel(D, R, share, mine, masks, steer, unit, gram):
    lane = lax.broadcasted_iota(jnp.int32, (CH, 128), 1)
    sign = jnp.where(lane < 64, -1.0, 1.0).astype(bf16)
    gram[...] = jnp.zeros_like(gram)

    def add(g, c):
        rows = masks[g].astype(f32)
        plain = [[mine[g * D + s, b] for s in range(D)] for b in range(share + 2)]
        turned = [[pltpu.roll(x.astype(f32), 64, 1).astype(bf16) * sign for x in line] for line in plain]
        plain_k = [jnp.concatenate(line, axis=1) for line in plain]
        turned_k = [jnp.concatenate(line, axis=1) for line in turned]
        for b in range(share):
            weight = jnp.concatenate(
                [jnp.broadcast_to(rows[b * D + s:b * D + s + 1], (CH, 128)).astype(bf16)
                 for s in range(D)], axis=1)
            left = jnp.concatenate([plain_k[b + i] * weight for i in range(3)], axis=0)
            right = jnp.concatenate(
                [plain_k[b + i] for i in range(3)] + [turned_k[b + i] for i in range(3)], axis=0)
            gram[b] += lax.dot_general(
                left, right, (((1,), (1,)), ((), ())), preferred_element_type=f32)
        return c

    lax.fori_loop(0, R, add, 0)

    eye_r = lax.broadcasted_iota(jnp.int32, (3 * CH, 6 * CH), 0)
    eye_c = lax.broadcasted_iota(jnp.int32, (3 * CH, 6 * CH), 1)
    diagonal = eye_r == eye_c
    cov = []
    for b in range(share):
        whole = gram[b]
        trace = jnp.sum(jnp.where(diagonal, whole, 0.0), keepdims=True)
        power = trace / (3 * CH) + epsilon
        whole = whole / power + jnp.where(diagonal, loading, 0.0)
        cov.append([[
            stacked_form(whole[i * CH:(i + 1) * CH, j * CH:(j + 1) * CH],
                         whole[i * CH:(i + 1) * CH, (3 + j) * CH:(4 + j) * CH])
            for j in range(3)] for i in range(3)])
    every = range(share)
    inverse0 = invert_all([cov[b][0][0] for b in every])
    ahead = [mul(full_form(inverse0[b]), jnp.concatenate([cov[b][0][1], cov[b][0][2]], axis=1))
             for b in every]
    down = [mul(jnp.concatenate([full_form(cov[b][1][0]), full_form(cov[b][2][0])], axis=0), ahead[b])
            for b in every]
    c11 = [cov[b][1][1] - down[b][:2 * CH, :CH] for b in every]
    c12 = [cov[b][1][2] - down[b][:2 * CH, CH:] for b in every]
    c21 = [cov[b][2][1] - down[b][2 * CH:, :CH] for b in every]
    inverse2 = invert_all([cov[b][2][2] - down[b][2 * CH:, CH:] for b in every])
    back = [mul(full_form(inverse2[b]), c21[b]) for b in every]
    inverse1 = invert_all([c11[b] - mul(full_form(c12[b]), back[b]) for b in every])
    steer_here = steer[...]
    for b in every:
        x1 = mul(full_form(inverse1[b]), steer_here)
        x2 = -mul(full_form(back[b]), x1)
        x0 = -(mul(full_form(ahead[b][:, :CH]), x1) + mul(full_form(ahead[b][:, CH:]), x2))
        gain = jnp.sum(steer_here * x1, axis=0, keepdims=True)
        scale = 1.0 / jnp.sqrt(gain)
        parts = [x * scale for x in (x0, x1, x2)]
        unit[b] = jnp.concatenate(
            [jnp.concatenate([x[:CH], x[CH:]], axis=1) for x in parts], axis=0).astype(bf16)


def beams_kernel(D, step_bins, wide, unit, out):
    first = pl.program_id(0) * step_bins
    lane = lax.broadcasted_iota(jnp.int32, (CH, 128), 1)
    sign = jnp.where(lane < 64, 1.0, -1.0).astype(bf16)
    rows = []
    for b in range(step_bins + 2):
        pieces = [wide[s, first + b] for s in range(D)]
        rows.append(jnp.concatenate([x[:, :64] for x in pieces], axis=1))
        rows.append(jnp.concatenate([x[:, 64:] for x in pieces], axis=1))
    for b in range(step_bins):
        weight = []
        for i in range(3):
            u = unit[b, i * CH:(i + 1) * CH]
            weight.append(u * sign)
            weight.append(pltpu.roll(u.astype(f32), 64, 1).astype(bf16))
        out[b] = lax.dot_general(
            jnp.concatenate(weight, axis=0), jnp.concatenate(rows[2 * b:2 * b + 6], axis=0),
            (((0,), (0,)), ((), ())), preferred_element_type=f32)


def body(echoes, training, look_index):
    D, R = lax.axis_size("dop"), lax.axis_size("rng")
    N = D * R
    bins = PULSES // D
    share = bins // R
    cells = echoes.shape[0]
    spec = jnp.einsum("qkQp,rQcp->kcqr", twiddle_table(), echoes, preferred_element_type=f32)
    spec = spec.astype(bf16).reshape(PULSES + 2, CH, 2 * cells)
    mask = training.astype(bf16).reshape(R, share, D, 1, cells)
    mask = jnp.broadcast_to(mask, (R, share, D, 2, cells)).reshape(R, share * D, 2 * cells)
    mask = jnp.pad(mask, ((0, 0), (0, -share * D % 16), (0, 0)))
    steer = steering(look_index)
    anywhere = pl.BlockSpec(memory_space=pl.ANY)
    in_vmem = pl.BlockSpec(memory_space=pltpu.VMEM)
    dma = pltpu.SemaphoreType.DMA
    wide, mine, masks = pl.pallas_call(
        functools.partial(exchange_kernel, D, R),
        out_shape=[
            jax.ShapeDtypeStruct((D, bins + 2, CH, 2 * cells), bf16),
            jax.ShapeDtypeStruct((N, share + 2, CH, 2 * cells), bf16),
            jax.ShapeDtypeStruct(mask.shape, bf16),
        ],
        in_specs=[anywhere] * 2,
        out_specs=[anywhere] * 3,
        scratch_shapes=[dma((R,)), dma((R,)), dma((N,)), dma((N,)), dma((D,)), dma((D,)), dma((3,))],
        compiler_params=pltpu.CompilerParams(collective_id=0, has_side_effects=True),
        name="exchange",
    )(spec, mask)
    unit = pl.pallas_call(
        functools.partial(weights_kernel, D, R, share),
        out_shape=jax.ShapeDtypeStruct((share, 3 * CH, 2 * LOOKS), bf16),
        in_specs=[in_vmem] * 3,
        out_specs=in_vmem,
        scratch_shapes=[pltpu.VMEM((share, 3 * CH, 6 * CH), f32)],
        compiler_params=pltpu.CompilerParams(vmem_limit_bytes=32 * 1024 * 1024),
        name="weights",
    )(mine, masks, steer)
    units = pl.pallas_call(
        functools.partial(gather_kernel, R),
        out_shape=jax.ShapeDtypeStruct((R,) + unit.shape, bf16),
        in_specs=[anywhere],
        out_specs=anywhere,
        scratch_shapes=[dma((R,)), dma((R,)), dma],
        compiler_params=pltpu.CompilerParams(collective_id=1, has_side_effects=True),
        name="gather",
    )(unit)
    units = units.reshape(bins, 3 * CH, 2 * LOOKS)
    step_bins = 4
    out = pl.pallas_call(
        functools.partial(beams_kernel, D, step_bins),
        grid=(bins // step_bins,),
        out_shape=jax.ShapeDtypeStruct((bins, 2 * LOOKS, D * cells), f32),
        in_specs=[
            in_vmem,
            pl.BlockSpec((step_bins, 3 * CH, 2 * LOOKS), lambda i: (i, 0, 0)),
        ],
        out_specs=pl.BlockSpec((step_bins, 2 * LOOKS, D * cells), lambda i: (i, 0, 0)),
        compiler_params=pltpu.CompilerParams(vmem_limit_bytes=32 * 1024 * 1024),
        name="beams",
    )(wide, units)
    return out.reshape(bins, 2, LOOKS, D * cells)


def solution(mesh):
    in_specs = (P(("rng", "dop"), None, None, None), P("dop", "rng"), P())
    out_specs = P("dop", None, None, "rng")
    return jax.shard_map(body, mesh=mesh, in_specs=in_specs, out_specs=out_specs, check_vma=False)
```

```python
import functools

import jax
import jax.numpy as jnp
import numpy as np
from jax import lax
from jax.experimental import pallas as pl
from jax.experimental.pallas import tpu as pltpu
from jax.sharding import PartitionSpec as P

CH = 32
PULSES = 128
LOOKS = 64
ANGLES = 256

loading = 0.1
epsilon = 1e-06
highest = lax.Precision.HIGHEST
MESH = pl.DeviceIdType.MESH
bf16 = jnp.bfloat16
f32 = jnp.float32


def twiddle_table(rows):
    pulse_ids = np.arange(PULSES)
    bins = np.arange(-1, rows - 1) % PULSES
    angles = ((bins[:, None] * pulse_ids[None, :]) % PULSES).astype(np.float32) * np.float32(
        2.0 * np.pi / PULSES
    )
    return jnp.asarray(np.concatenate([np.cos(angles), np.sin(angles)], axis=1), bf16)


def spectra_kernel(group, echoes, table, spec):
    left = table[...]
    for first in range(0, CH, group):
        real, imag = [
            jnp.swapaxes(echoes[:, q, first:first + group].astype(f32), 0, 1).astype(bf16)
            for q in range(2)
        ]
        planes = []
        for c in range(group):
            right = jnp.concatenate(
                [jnp.concatenate([real[c], imag[c]], axis=1),
                 jnp.concatenate([imag[c], -real[c]], axis=1)], axis=0)
            planes.append(lax.dot_general(
                left, right, (((1,), (1,)), ((), ())), preferred_element_type=f32))
        turned = jnp.swapaxes(jnp.stack(planes), 0, 1)
        spec[:, first:first + group] = turned.astype(bf16)


def steering(look_index):
    sines = -1.0 + (2.0 * look_index.astype(f32) + 1.0) / ANGLES
    channel_ids = jnp.arange(CH).astype(f32)
    phases = jnp.pi * channel_ids[:, None] * sines[None, :]
    return jnp.concatenate([jnp.cos(phases), jnp.sin(phases)], axis=0)


def exchange_kernel(D, R, spec, mask, wide, mine, masks, send_m, recv_m, send_x, recv_x,
                    send_w, recv_w, own):
    N = D * R
    bins = PULSES // D
    share = bins // R
    d, g = lax.axis_index("dop"), lax.axis_index("rng")
    me = g * D + d
    barrier = pltpu.get_barrier_semaphore()

    def where(j):
        t = lax.rem(me + j, N)
        return t, lax.rem(t, D), t // D

    def greet(j, c):
        _, td, tg = where(j)
        pl.semaphore_signal(barrier, inc=1, device_id=(td, tg), device_id_type=MESH)
        return c

    lax.fori_loop(1, N, greet, 0)
    local = [
        pltpu.make_async_copy(mask.at[g], masks.at[g], own.at[0]),
        pltpu.make_async_copy(spec.at[pl.ds(d * bins + g * share, share + 2)], mine.at[me], own.at[1]),
        pltpu.make_async_copy(spec.at[pl.ds(d * bins, bins + 2)], wide.at[d], own.at[2]),
    ]
    for copy in local:
        copy.start()
    pl.semaphore_wait(barrier, N - 1)

    def mask_copy(j):
        tg = lax.rem(g + j, R)
        return pltpu.make_async_remote_copy(
            mask.at[tg], masks.at[g], send_m.at[j], recv_m.at[g], device_id=(d, tg),
            device_id_type=MESH)

    def mine_copy(j):
        _, td, tg = where(j)
        return pltpu.make_async_remote_copy(
            spec.at[pl.ds(td * bins + tg * share, share + 2)], mine.at[me], send_x.at[j],
            recv_x.at[me], device_id=(td, tg), device_id_type=MESH)

    def wide_copy(j):
        td = lax.rem(d + j, D)
        return pltpu.make_async_remote_copy(
            spec.at[pl.ds(td * bins, bins + 2)], wide.at[d], send_w.at[j], recv_w.at[d],
            device_id=(td, g), device_id_type=MESH)

    def start(make):
        def run(j, c):
            make(j).start()
            return c
        return run

    lax.fori_loop(1, R, start(mask_copy), 0)
    lax.fori_loop(1, N, start(mine_copy), 0)
    lax.fori_loop(1, D, start(wide_copy), 0)

    def end_mask(j, c):
        src = lax.rem(g + j, R)
        mask_copy(j).wait_send()
        pltpu.make_async_remote_copy(
            mask.at[0], masks.at[src], send_m.at[j], recv_m.at[src], device_id=(d, src),
            device_id_type=MESH).wait_recv()
        return c

    def end_mine(j, c):
        src, sd, sg = where(j)
        mine_copy(j).wait_send()
        pltpu.make_async_remote_copy(
            spec.at[pl.ds(0, share + 2)], mine.at[src], send_x.at[j], recv_x.at[src],
            device_id=(sd, sg), device_id_type=MESH).wait_recv()
        return c

    def end_wide(j, c):
        src = lax.rem(d + j, D)
        wide_copy(j).wait_send()
        pltpu.make_async_remote_copy(
            spec.at[pl.ds(0, bins + 2)], wide.at[src], send_w.at[j], recv_w.at[src],
            device_id=(src, g), device_id_type=MESH).wait_recv()
        return c

    lax.fori_loop(1, R, end_mask, 0)
    lax.fori_loop(1, N, end_mine, 0)
    lax.fori_loop(1, D, end_wide, 0)
    for copy in local:
        copy.wait()


def gather_kernel(R, unit, out, send, recv, pass_on, own):
    H = R // 2
    d, g = lax.axis_index("dop"), lax.axis_index("rng")
    half = g // H * H
    partner = lax.rem(g + H, R)
    other = H - half
    barrier = pltpu.get_barrier_semaphore()

    def peer(j):
        return half + lax.rem(g - half + j, H)

    def greet(j, c):
        pl.semaphore_signal(barrier, inc=1, device_id=(d, peer(j)), device_id_type=MESH)
        return c

    lax.fori_loop(1, H, greet, 0)
    pl.semaphore_signal(barrier, inc=1, device_id=(d, partner), device_id_type=MESH)
    local = pltpu.make_async_copy(unit, out.at[g], own)
    local.start()
    pl.semaphore_wait(barrier, H)

    cross = pltpu.make_async_remote_copy(
        unit, out.at[g], send.at[0], recv.at[g], device_id=(d, partner), device_id_type=MESH)
    cross.start()

    def make(j):
        return pltpu.make_async_remote_copy(
            unit, out.at[g], send.at[j], recv.at[g], device_id=(d, peer(j)), device_id_type=MESH)

    def hand(j):
        return pltpu.make_async_remote_copy(
            out.at[partner], out.at[partner], pass_on.at[j], recv.at[partner],
            device_id=(d, peer(j)), device_id_type=MESH)

    def arrive(src):
        pltpu.make_async_remote_copy(
            unit, out.at[src], send.at[0], recv.at[src], device_id=(d, partner),
            device_id_type=MESH).wait_recv()

    def begin(j, c):
        make(j).start()
        return c

    def begin_hand(j, c):
        hand(j).start()
        return c

    def end(j, c):
        make(j).wait_send()
        hand(j).wait_send()
        arrive(peer(j))
        arrive(other + lax.rem(g - half + j, H))
        return c

    lax.fori_loop(1, H, begin, 0)
    arrive(partner)
    lax.fori_loop(1, H, begin_hand, 0)
    lax.fori_loop(1, H, end, 0)
    cross.wait_send()
    local.wait()


def invert(re, im):
    width = re.shape[1]
    lane = lax.broadcasted_iota(jnp.int32, (CH, width), 1)
    row = lax.broadcasted_iota(jnp.int32, (CH, width), 0)
    base = lane // CH * CH
    col = lane - base
    for k in range(CH):
        pick = base + k
        cr = jnp.take_along_axis(re, pick, axis=1)
        ci = jnp.take_along_axis(im, pick, axis=1)
        at_col, at_row = col == k, row == k
        scale = 1.0 / cr[k:k + 1]
        rr = jnp.where(at_col[:1], 1.0, re[k:k + 1]) * scale
        ri = jnp.where(at_col[:1], 0.0, im[k:k + 1]) * scale
        clear = jnp.logical_or(at_col, at_row)
        cr = jnp.where(at_row, -1.0, cr)
        ci = jnp.where(at_row, 0.0, ci)
        re = jnp.where(clear, 0.0, re) - (cr * rr - ci * ri)
        im = jnp.where(clear, 0.0, im) - (cr * ri + ci * rr)
    return re, im


def stacked_form(re, im):
    return jnp.concatenate([re, im], axis=0)


def full_form(stacked):
    re, im = stacked[:CH], stacked[CH:]
    return jnp.concatenate(
        [jnp.concatenate([re, -im], axis=1), jnp.concatenate([im, re], axis=1)], axis=0)


def mul(a, b):
    return jnp.dot(a, b, precision=highest, preferred_element_type=f32)


def invert_all(blocks):
    lanes = 128 // CH
    packed = (blocks * lanes)[:lanes] if len(blocks) < lanes else blocks
    re, im = invert(
        jnp.concatenate([block[:CH] for block in packed], axis=1),
        jnp.concatenate([block[CH:] for block in packed], axis=1))
    return [
        stacked_form(re[:, i * CH:(i + 1) * CH], im[:, i * CH:(i + 1) * CH])
        for i in range(len(blocks))
    ]


def weights_kernel(D, R, share, mine, masks, steer, unit, gram):
    lane = lax.broadcasted_iota(jnp.int32, (CH, 128), 1)
    sign = jnp.where(lane < 64, -1.0, 1.0).astype(bf16)
    gram[...] = jnp.zeros_like(gram)

    def add(g, c):
        rows = masks[g].astype(f32)
        plain = [[mine[g * D + s, b] for s in range(D)] for b in range(share + 2)]
        turned = [[pltpu.roll(x.astype(f32), 64, 1).astype(bf16) * sign for x in line] for line in plain]
        plain_k = [jnp.concatenate(line, axis=1) for line in plain]
        turned_k = [jnp.concatenate(line, axis=1) for line in turned]
        for b in range(share):
            weight = jnp.concatenate(
                [jnp.broadcast_to(rows[b * D + s:b * D + s + 1], (CH, 128)).astype(bf16)
                 for s in range(D)], axis=1)
            left = jnp.concatenate([plain_k[b + i] * weight for i in range(3)], axis=0)
            right = jnp.concatenate(
                [plain_k[b + i] for i in range(3)] + [turned_k[b + i] for i in range(3)], axis=0)
            gram[b] += lax.dot_general(
                left, right, (((1,), (1,)), ((), ())), preferred_element_type=f32)
        return c

    lax.fori_loop(0, R, add, 0)

    eye_r = lax.broadcasted_iota(jnp.int32, (3 * CH, 6 * CH), 0)
    eye_c = lax.broadcasted_iota(jnp.int32, (3 * CH, 6 * CH), 1)
    diagonal = eye_r == eye_c
    cov = []
    for b in range(share):
        whole = gram[b]
        trace = jnp.sum(jnp.where(diagonal, whole, 0.0), keepdims=True)
        power = trace / (3 * CH) + epsilon
        whole = whole / power + jnp.where(diagonal, loading, 0.0)
        cov.append([[
            stacked_form(whole[i * CH:(i + 1) * CH, j * CH:(j + 1) * CH],
                         whole[i * CH:(i + 1) * CH, (3 + j) * CH:(4 + j) * CH])
            for j in range(3)] for i in range(3)])
    every = range(share)
    inverse0 = invert_all([cov[b][0][0] for b in every])
    ahead = [mul(full_form(inverse0[b]), jnp.concatenate([cov[b][0][1], cov[b][0][2]], axis=1))
             for b in every]
    down = [mul(jnp.concatenate([full_form(cov[b][1][0]), full_form(cov[b][2][0])], axis=0), ahead[b])
            for b in every]
    c11 = [cov[b][1][1] - down[b][:2 * CH, :CH] for b in every]
    c12 = [cov[b][1][2] - down[b][:2 * CH, CH:] for b in every]
    c21 = [cov[b][2][1] - down[b][2 * CH:, :CH] for b in every]
    inverse2 = invert_all([cov[b][2][2] - down[b][2 * CH:, CH:] for b in every])
    back = [mul(full_form(inverse2[b]), c21[b]) for b in every]
    inverse1 = invert_all([c11[b] - mul(full_form(c12[b]), back[b]) for b in every])
    steer_here = steer[...]
    for b in every:
        x1 = mul(full_form(inverse1[b]), steer_here)
        x2 = -mul(full_form(back[b]), x1)
        x0 = -(mul(full_form(ahead[b][:, :CH]), x1) + mul(full_form(ahead[b][:, CH:]), x2))
        gain = jnp.sum(steer_here * x1, axis=0, keepdims=True)
        scale = 1.0 / jnp.sqrt(gain)
        parts = [x * scale for x in (x0, x1, x2)]
        unit[b] = jnp.concatenate(
            [jnp.concatenate([x[:CH], x[CH:]], axis=1) for x in parts], axis=0).astype(bf16)


def beams_kernel(D, step_bins, wide, unit, out):
    first = pl.program_id(0) * step_bins
    lane = lax.broadcasted_iota(jnp.int32, (CH, 128), 1)
    sign = jnp.where(lane < 64, 1.0, -1.0).astype(bf16)
    rows = []
    for b in range(step_bins + 2):
        pieces = [wide[s, first + b] for s in range(D)]
        rows.append(jnp.concatenate([x[:, :64] for x in pieces], axis=1))
        rows.append(jnp.concatenate([x[:, 64:] for x in pieces], axis=1))
    for b in range(step_bins):
        weight = []
        for i in range(3):
            u = unit[b, i * CH:(i + 1) * CH]
            weight.append(u * sign)
            weight.append(pltpu.roll(u.astype(f32), 64, 1).astype(bf16))
        out[b] = lax.dot_general(
            jnp.concatenate(weight, axis=0), jnp.concatenate(rows[2 * b:2 * b + 6], axis=0),
            (((0,), (0,)), ((), ())), preferred_element_type=f32)


def body(echoes, training, look_index):
    D, R = lax.axis_size("dop"), lax.axis_size("rng")
    N = D * R
    bins = PULSES // D
    share = bins // R
    cells = echoes.shape[0]
    rows = PULSES + 8
    mask = training.astype(bf16).reshape(R, share, D, 1, cells)
    mask = jnp.broadcast_to(mask, (R, share, D, 2, cells)).reshape(R, share * D, 2 * cells)
    mask = jnp.pad(mask, ((0, 0), (0, -share * D % 16), (0, 0)))
    steer = steering(look_index)
    anywhere = pl.BlockSpec(memory_space=pl.ANY)
    in_vmem = pl.BlockSpec(memory_space=pltpu.VMEM)
    dma = pltpu.SemaphoreType.DMA
    spec = pl.pallas_call(
        functools.partial(spectra_kernel, 16),
        out_shape=jax.ShapeDtypeStruct((rows, CH, 2 * cells), bf16),
        in_specs=[in_vmem] * 2,
        out_specs=in_vmem,
        compiler_params=pltpu.CompilerParams(vmem_limit_bytes=32 * 1024 * 1024),
        name="spectra",
    )(echoes, twiddle_table(rows))
    wide, mine, masks = pl.pallas_call(
        functools.partial(exchange_kernel, D, R),
        out_shape=[
            jax.ShapeDtypeStruct((D, bins + 2, CH, 2 * cells), bf16),
            jax.ShapeDtypeStruct((N, share + 2, CH, 2 * cells), bf16),
            jax.ShapeDtypeStruct(mask.shape, bf16),
        ],
        in_specs=[anywhere] * 2,
        out_specs=[anywhere] * 3,
        scratch_shapes=[dma((R,)), dma((R,)), dma((N,)), dma((N,)), dma((D,)), dma((D,)), dma((3,))],
        compiler_params=pltpu.CompilerParams(collective_id=0, has_side_effects=True),
        name="exchange",
    )(spec, mask)
    unit = pl.pallas_call(
        functools.partial(weights_kernel, D, R, share),
        out_shape=jax.ShapeDtypeStruct((share, 3 * CH, 2 * LOOKS), bf16),
        in_specs=[in_vmem] * 3,
        out_specs=in_vmem,
        scratch_shapes=[pltpu.VMEM((share, 3 * CH, 6 * CH), f32)],
        compiler_params=pltpu.CompilerParams(vmem_limit_bytes=32 * 1024 * 1024),
        name="weights",
    )(mine, masks, steer)
    units = pl.pallas_call(
        functools.partial(gather_kernel, R),
        out_shape=jax.ShapeDtypeStruct((R,) + unit.shape, bf16),
        in_specs=[anywhere],
        out_specs=anywhere,
        scratch_shapes=[dma((R,)), dma((R,)), dma((R,)), dma],
        compiler_params=pltpu.CompilerParams(collective_id=1, has_side_effects=True),
        name="gather",
    )(unit)
    units = units.reshape(bins, 3 * CH, 2 * LOOKS)
    step_bins = 4
    out = pl.pallas_call(
        functools.partial(beams_kernel, D, step_bins),
        grid=(bins // step_bins,),
        out_shape=jax.ShapeDtypeStruct((bins, 2 * LOOKS, D * cells), f32),
        in_specs=[
            in_vmem,
            pl.BlockSpec((step_bins, 3 * CH, 2 * LOOKS), lambda i: (i, 0, 0)),
        ],
        out_specs=pl.BlockSpec((step_bins, 2 * LOOKS, D * cells), lambda i: (i, 0, 0)),
        compiler_params=pltpu.CompilerParams(vmem_limit_bytes=32 * 1024 * 1024),
        name="beams",
    )(wide, units)
    return out.reshape(bins, 2, LOOKS, D * cells)


def solution(mesh):
    in_specs = (P(("rng", "dop"), None, None, None), P("dop", "rng"), P())
    out_specs = P("dop", None, None, "rng")
    return jax.shard_map(body, mesh=mesh, in_specs=in_specs, out_specs=out_specs, check_vma=False)
```

```python
import functools

import jax
import jax.numpy as jnp
import numpy as np
from jax import lax
from jax.experimental import pallas as pl
from jax.experimental.pallas import tpu as pltpu
from jax.sharding import PartitionSpec as P

CH = 32
PULSES = 128
LOOKS = 64
ANGLES = 256

loading = 0.1
epsilon = 1e-06
highest = lax.Precision.HIGHEST
MESH = pl.DeviceIdType.MESH
bf16 = jnp.bfloat16
f32 = jnp.float32


def twiddle_table(rows):
    pulse_ids = np.arange(PULSES)
    bins = np.arange(-1, rows - 1) % PULSES
    angles = ((bins[:, None] * pulse_ids[None, :]) % PULSES).astype(np.float32) * np.float32(
        2.0 * np.pi / PULSES
    )
    return jnp.asarray(np.concatenate([np.cos(angles), np.sin(angles)], axis=1), bf16)


def spectra_kernel(group, echoes, table, spec):
    left = table[...]
    for first in range(0, CH, group):
        real, imag = [
            jnp.swapaxes(echoes[:, q, first:first + group].astype(f32), 0, 1).astype(bf16)
            for q in range(2)
        ]
        planes = []
        for c in range(group):
            right = jnp.concatenate(
                [jnp.concatenate([real[c], imag[c]], axis=1),
                 jnp.concatenate([imag[c], -real[c]], axis=1)], axis=0)
            planes.append(lax.dot_general(
                left, right, (((1,), (1,)), ((), ())), preferred_element_type=f32))
        turned = jnp.swapaxes(jnp.stack(planes), 0, 1)
        spec[:, first:first + group] = turned.astype(bf16)


def steering(look_index):
    sines = -1.0 + (2.0 * look_index.astype(f32) + 1.0) / ANGLES
    channel_ids = jnp.arange(CH).astype(f32)
    phases = jnp.pi * channel_ids[:, None] * sines[None, :]
    return jnp.concatenate([jnp.cos(phases), jnp.sin(phases)], axis=0)


def exchange_kernel(D, R, spec, mask, mine, masks, send_m, recv_m, send_x, recv_x,
                    own):
    N = D * R
    bins = PULSES // D
    share = bins // R
    d, g = lax.axis_index("dop"), lax.axis_index("rng")
    me = g * D + d
    barrier = pltpu.get_barrier_semaphore()

    def where(j):
        t = lax.rem(me + j, N)
        return t, lax.rem(t, D), t // D

    def greet(j, c):
        _, td, tg = where(j)
        pl.semaphore_signal(barrier, inc=1, device_id=(td, tg), device_id_type=MESH)
        return c

    lax.fori_loop(1, N, greet, 0)
    local = [
        pltpu.make_async_copy(mask.at[g], masks.at[g], own.at[0]),
        pltpu.make_async_copy(spec.at[pl.ds(d * bins + g * share, share + 2)], mine.at[me], own.at[1]),
    ]
    for copy in local:
        copy.start()
    pl.semaphore_wait(barrier, N - 1)

    def mask_copy(j):
        tg = lax.rem(g + j, R)
        return pltpu.make_async_remote_copy(
            mask.at[tg], masks.at[g], send_m.at[j], recv_m.at[g], device_id=(d, tg),
            device_id_type=MESH)

    def mine_copy(j):
        _, td, tg = where(j)
        return pltpu.make_async_remote_copy(
            spec.at[pl.ds(td * bins + tg * share, share + 2)], mine.at[me], send_x.at[j],
            recv_x.at[me], device_id=(td, tg), device_id_type=MESH)

    def start(make):
        def run(j, c):
            make(j).start()
            return c
        return run

    lax.fori_loop(1, R, start(mask_copy), 0)
    lax.fori_loop(1, N, start(mine_copy), 0)

    def end_mask(j, c):
        src = lax.rem(g + j, R)
        mask_copy(j).wait_send()
        pltpu.make_async_remote_copy(
            mask.at[0], masks.at[src], send_m.at[j], recv_m.at[src], device_id=(d, src),
            device_id_type=MESH).wait_recv()
        return c

    def end_mine(j, c):
        src, sd, sg = where(j)
        mine_copy(j).wait_send()
        pltpu.make_async_remote_copy(
            spec.at[pl.ds(0, share + 2)], mine.at[src], send_x.at[j], recv_x.at[src],
            device_id=(sd, sg), device_id_type=MESH).wait_recv()
        return c

    lax.fori_loop(1, R, end_mask, 0)
    lax.fori_loop(1, N, end_mine, 0)
    for copy in local:
        copy.wait()


def gather_kernel(D, R, share, unit, spec, out, wide, send, recv, cross_send, cross_recv, hand_send,
                  hand_recv, send_w, recv_w, own):
    H = R // 2
    bins = PULSES // D
    d, g = lax.axis_index("dop"), lax.axis_index("rng")
    half = g // H * H
    partner = lax.rem(g + H, R)
    other = H - half
    barrier = pltpu.get_barrier_semaphore()

    def peer(j):
        return half + lax.rem(g - half + j, H)

    def greet(j, c):
        pl.semaphore_signal(barrier, inc=1, device_id=(d, peer(j)), device_id_type=MESH)
        return c

    def greet_dop(j, c):
        pl.semaphore_signal(barrier, inc=1, device_id=(lax.rem(d + j, D), g), device_id_type=MESH)
        return c

    lax.fori_loop(1, H, greet, 0)
    lax.fori_loop(1, D, greet_dop, 0)
    pl.semaphore_signal(barrier, inc=1, device_id=(d, partner), device_id_type=MESH)
    local = [
        pltpu.make_async_copy(unit, out.at[g], own.at[0]),
        pltpu.make_async_copy(spec.at[pl.ds(d * bins, bins + 2)], wide.at[d], own.at[1]),
    ]
    for copy in local:
        copy.start()
    pl.semaphore_wait(barrier, H + D - 1)

    def cross(b):
        return pltpu.make_async_remote_copy(
            unit.at[b], out.at[g, b], cross_send.at[b], cross_recv.at[b], device_id=(d, partner),
            device_id_type=MESH)

    def make(j):
        return pltpu.make_async_remote_copy(
            unit, out.at[g], send.at[j], recv.at[g], device_id=(d, peer(j)), device_id_type=MESH)

    def hand(j, b):
        return pltpu.make_async_remote_copy(
            out.at[partner, b], out.at[partner, b], hand_send.at[j, b], hand_recv.at[partner, b],
            device_id=(d, peer(j)), device_id_type=MESH)

    def wide_copy(j):
        td = lax.rem(d + j, D)
        return pltpu.make_async_remote_copy(
            spec.at[pl.ds(td * bins, bins + 2)], wide.at[d], send_w.at[j], recv_w.at[d],
            device_id=(td, g), device_id_type=MESH)

    def begin(j, c):
        make(j).start()
        return c

    def begin_wide(j, c):
        wide_copy(j).start()
        return c

    def end(j, c):
        make(j).wait_send()
        src = peer(j)
        pltpu.make_async_remote_copy(
            unit, out.at[src], send.at[j], recv.at[src], device_id=(d, src),
            device_id_type=MESH).wait_recv()
        far = other + lax.rem(g - half + j, H)
        for b in range(share):
            hand(j, b).wait_send()
            pltpu.make_async_remote_copy(
                unit.at[b], out.at[far, b], hand_send.at[j, b], hand_recv.at[far, b],
                device_id=(d, src), device_id_type=MESH).wait_recv()
        return c

    def end_wide(j, c):
        src = lax.rem(d + j, D)
        wide_copy(j).wait_send()
        pltpu.make_async_remote_copy(
            spec.at[pl.ds(0, bins + 2)], wide.at[src], send_w.at[j], recv_w.at[src],
            device_id=(src, g), device_id_type=MESH).wait_recv()
        return c

    for b in range(share):
        cross(b).start()
    lax.fori_loop(1, H, begin, 0)
    lax.fori_loop(1, D, begin_wide, 0)
    for b in range(share):
        pltpu.make_async_remote_copy(
            unit.at[b], out.at[partner, b], cross_send.at[b], cross_recv.at[b],
            device_id=(d, partner), device_id_type=MESH).wait_recv()

        def begin_hand(j, c):
            hand(j, b).start()
            return c

        lax.fori_loop(1, H, begin_hand, 0)
    lax.fori_loop(1, H, end, 0)
    lax.fori_loop(1, D, end_wide, 0)
    for b in range(share):
        cross(b).wait_send()
    for copy in local:
        copy.wait()


def invert(re, im):
    width = re.shape[1]
    lane = lax.broadcasted_iota(jnp.int32, (CH, width), 1)
    row = lax.broadcasted_iota(jnp.int32, (CH, width), 0)
    base = lane // CH * CH
    col = lane - base
    for k in range(CH):
        pick = base + k
        cr = jnp.take_along_axis(re, pick, axis=1)
        ci = jnp.take_along_axis(im, pick, axis=1)
        at_col, at_row = col == k, row == k
        scale = 1.0 / cr[k:k + 1]
        rr = jnp.where(at_col[:1], 1.0, re[k:k + 1]) * scale
        ri = jnp.where(at_col[:1], 0.0, im[k:k + 1]) * scale
        clear = jnp.logical_or(at_col, at_row)
        cr = jnp.where(at_row, -1.0, cr)
        ci = jnp.where(at_row, 0.0, ci)
        re = jnp.where(clear, 0.0, re) - (cr * rr - ci * ri)
        im = jnp.where(clear, 0.0, im) - (cr * ri + ci * rr)
    return re, im


def stacked_form(re, im):
    return jnp.concatenate([re, im], axis=0)


def full_form(stacked):
    re, im = stacked[:CH], stacked[CH:]
    return jnp.concatenate(
        [jnp.concatenate([re, -im], axis=1), jnp.concatenate([im, re], axis=1)], axis=0)


def mul(a, b):
    return jnp.dot(a, b, precision=highest, preferred_element_type=f32)


def invert_all(blocks):
    lanes = 128 // CH
    packed = (blocks * lanes)[:lanes] if len(blocks) < lanes else blocks
    re, im = invert(
        jnp.concatenate([block[:CH] for block in packed], axis=1),
        jnp.concatenate([block[CH:] for block in packed], axis=1))
    return [
        stacked_form(re[:, i * CH:(i + 1) * CH], im[:, i * CH:(i + 1) * CH])
        for i in range(len(blocks))
    ]


def weights_kernel(D, R, share, mine, masks, steer, unit, gram):
    lane = lax.broadcasted_iota(jnp.int32, (CH, 128), 1)
    sign = jnp.where(lane < 64, -1.0, 1.0).astype(bf16)
    gram[...] = jnp.zeros_like(gram)

    def add(g, c):
        rows = masks[g].astype(f32)
        plain = [[mine[g * D + s, b] for s in range(D)] for b in range(share + 2)]
        turned = [[pltpu.roll(x.astype(f32), 64, 1).astype(bf16) * sign for x in line] for line in plain]
        plain_k = [jnp.concatenate(line, axis=1) for line in plain]
        turned_k = [jnp.concatenate(line, axis=1) for line in turned]
        for b in range(share):
            weight = jnp.concatenate(
                [jnp.broadcast_to(rows[b * D + s:b * D + s + 1], (CH, 128)).astype(bf16)
                 for s in range(D)], axis=1)
            left = jnp.concatenate([plain_k[b + i] * weight for i in range(3)], axis=0)
            right = jnp.concatenate(
                [plain_k[b + i] for i in range(3)] + [turned_k[b + i] for i in range(3)], axis=0)
            gram[b] += lax.dot_general(
                left, right, (((1,), (1,)), ((), ())), preferred_element_type=f32)
        return c

    lax.fori_loop(0, R, add, 0)

    eye_r = lax.broadcasted_iota(jnp.int32, (3 * CH, 6 * CH), 0)
    eye_c = lax.broadcasted_iota(jnp.int32, (3 * CH, 6 * CH), 1)
    diagonal = eye_r == eye_c
    cov = []
    for b in range(share):
        whole = gram[b]
        trace = jnp.sum(jnp.where(diagonal, whole, 0.0), keepdims=True)
        power = trace / (3 * CH) + epsilon
        whole = whole / power + jnp.where(diagonal, loading, 0.0)
        cov.append([[
            stacked_form(whole[i * CH:(i + 1) * CH, j * CH:(j + 1) * CH],
                         whole[i * CH:(i + 1) * CH, (3 + j) * CH:(4 + j) * CH])
            for j in range(3)] for i in range(3)])
    every = range(share)
    inverse0 = invert_all([cov[b][0][0] for b in every])
    ahead = [mul(full_form(inverse0[b]), jnp.concatenate([cov[b][0][1], cov[b][0][2]], axis=1))
             for b in every]
    down = [mul(jnp.concatenate([full_form(cov[b][1][0]), full_form(cov[b][2][0])], axis=0), ahead[b])
            for b in every]
    c11 = [cov[b][1][1] - down[b][:2 * CH, :CH] for b in every]
    c12 = [cov[b][1][2] - down[b][:2 * CH, CH:] for b in every]
    c21 = [cov[b][2][1] - down[b][2 * CH:, :CH] for b in every]
    inverse2 = invert_all([cov[b][2][2] - down[b][2 * CH:, CH:] for b in every])
    back = [mul(full_form(inverse2[b]), c21[b]) for b in every]
    inverse1 = invert_all([c11[b] - mul(full_form(c12[b]), back[b]) for b in every])
    steer_here = steer[...]
    for b in every:
        x1 = mul(full_form(inverse1[b]), steer_here)
        x2 = -mul(full_form(back[b]), x1)
        x0 = -(mul(full_form(ahead[b][:, :CH]), x1) + mul(full_form(ahead[b][:, CH:]), x2))
        gain = jnp.sum(steer_here * x1, axis=0, keepdims=True)
        scale = 1.0 / jnp.sqrt(gain)
        parts = [x * scale for x in (x0, x1, x2)]
        unit[b] = jnp.concatenate(
            [jnp.concatenate([x[:CH], x[CH:]], axis=1) for x in parts], axis=0).astype(bf16)


def beams_kernel(D, step_bins, wide, unit, out):
    first = pl.program_id(0) * step_bins
    lane = lax.broadcasted_iota(jnp.int32, (CH, 128), 1)
    sign = jnp.where(lane < 64, 1.0, -1.0).astype(bf16)
    rows = []
    for b in range(step_bins + 2):
        pieces = [wide[s, first + b] for s in range(D)]
        rows.append(jnp.concatenate([x[:, :64] for x in pieces], axis=1))
        rows.append(jnp.concatenate([x[:, 64:] for x in pieces], axis=1))
    for b in range(step_bins):
        weight = []
        for i in range(3):
            u = unit[b, i * CH:(i + 1) * CH]
            weight.append(u * sign)
            weight.append(pltpu.roll(u.astype(f32), 64, 1).astype(bf16))
        out[b] = lax.dot_general(
            jnp.concatenate(weight, axis=0), jnp.concatenate(rows[2 * b:2 * b + 6], axis=0),
            (((0,), (0,)), ((), ())), preferred_element_type=f32)


def body(echoes, training, look_index):
    D, R = lax.axis_size("dop"), lax.axis_size("rng")
    N = D * R
    bins = PULSES // D
    share = bins // R
    cells = echoes.shape[0]
    rows = PULSES + 8
    mask = training.astype(bf16).reshape(R, share, D, 1, cells)
    mask = jnp.broadcast_to(mask, (R, share, D, 2, cells)).reshape(R, share * D, 2 * cells)
    mask = jnp.pad(mask, ((0, 0), (0, -share * D % 16), (0, 0)))
    steer = steering(look_index)
    anywhere = pl.BlockSpec(memory_space=pl.ANY)
    in_vmem = pl.BlockSpec(memory_space=pltpu.VMEM)
    dma = pltpu.SemaphoreType.DMA
    spec = pl.pallas_call(
        functools.partial(spectra_kernel, 16),
        out_shape=jax.ShapeDtypeStruct((rows, CH, 2 * cells), bf16),
        in_specs=[in_vmem] * 2,
        out_specs=in_vmem,
        compiler_params=pltpu.CompilerParams(vmem_limit_bytes=32 * 1024 * 1024),
        name="spectra",
    )(echoes, twiddle_table(rows))
    mine, masks = pl.pallas_call(
        functools.partial(exchange_kernel, D, R),
        out_shape=[
            jax.ShapeDtypeStruct((N, share + 2, CH, 2 * cells), bf16),
            jax.ShapeDtypeStruct(mask.shape, bf16),
        ],
        in_specs=[anywhere] * 2,
        out_specs=[anywhere] * 2,
        scratch_shapes=[dma((R,)), dma((R,)), dma((N,)), dma((N,)), dma((2,))],
        compiler_params=pltpu.CompilerParams(collective_id=0, has_side_effects=True),
        name="exchange",
    )(spec, mask)
    unit = pl.pallas_call(
        functools.partial(weights_kernel, D, R, share),
        out_shape=jax.ShapeDtypeStruct((share, 3 * CH, 2 * LOOKS), bf16),
        in_specs=[in_vmem] * 3,
        out_specs=in_vmem,
        scratch_shapes=[pltpu.VMEM((share, 3 * CH, 6 * CH), f32)],
        compiler_params=pltpu.CompilerParams(vmem_limit_bytes=32 * 1024 * 1024),
        name="weights",
    )(mine, masks, steer)
    units, wide = pl.pallas_call(
        functools.partial(gather_kernel, D, R, share),
        out_shape=[
            jax.ShapeDtypeStruct((R,) + unit.shape, bf16),
            jax.ShapeDtypeStruct((D, bins + 2, CH, 2 * cells), bf16),
        ],
        in_specs=[anywhere] * 2,
        out_specs=[anywhere] * 2,
        scratch_shapes=[
            dma((R,)), dma((R,)), dma((share,)), dma((share,)), dma((R, share)), dma((R, share)),
            dma((D,)), dma((D,)), dma((2,)),
        ],
        compiler_params=pltpu.CompilerParams(collective_id=1, has_side_effects=True),
        name="gather",
    )(unit, spec)
    units = units.reshape(bins, 3 * CH, 2 * LOOKS)
    step_bins = 4
    out = pl.pallas_call(
        functools.partial(beams_kernel, D, step_bins),
        grid=(bins // step_bins,),
        out_shape=jax.ShapeDtypeStruct((bins, 2 * LOOKS, D * cells), f32),
        in_specs=[
            in_vmem,
            pl.BlockSpec((step_bins, 3 * CH, 2 * LOOKS), lambda i: (i, 0, 0)),
        ],
        out_specs=pl.BlockSpec((step_bins, 2 * LOOKS, D * cells), lambda i: (i, 0, 0)),
        compiler_params=pltpu.CompilerParams(vmem_limit_bytes=32 * 1024 * 1024),
        name="beams",
    )(wide, units)
    return out.reshape(bins, 2, LOOKS, D * cells)


def solution(mesh):
    in_specs = (P(("rng", "dop"), None, None, None), P("dop", "rng"), P())
    out_specs = P("dop", None, None, "rng")
    return jax.shard_map(body, mesh=mesh, in_specs=in_specs, out_specs=out_specs, check_vma=False)
```

```python
import functools

import jax
import jax.numpy as jnp
import numpy as np
from jax import lax
from jax.experimental import pallas as pl
from jax.experimental.pallas import tpu as pltpu
from jax.sharding import PartitionSpec as P

CH = 32
PULSES = 128
LOOKS = 64
ANGLES = 256

loading = 0.1
epsilon = 1e-06
highest = lax.Precision.HIGHEST
MESH = pl.DeviceIdType.MESH
bf16 = jnp.bfloat16
f32 = jnp.float32


def twiddle_table(rows):
    pulse_ids = np.arange(PULSES)
    bins = np.arange(-1, rows - 1) % PULSES
    angles = ((bins[:, None] * pulse_ids[None, :]) % PULSES).astype(np.float32) * np.float32(
        2.0 * np.pi / PULSES
    )
    return jnp.asarray(np.concatenate([np.cos(angles), np.sin(angles)], axis=1), bf16)


def spectra_kernel(group, D, R, echoes, table, training, spec, mask):
    cells = echoes.shape[0]
    share = training.shape[0] // R
    trains = training[...].astype(f32)
    pieces = [trains[:, s * cells:(s + 1) * cells] for s in range(D)]
    pieces = [jnp.concatenate([piece, piece], axis=1) for piece in pieces]
    spare = jnp.zeros((-share * D % 16, 2 * cells), f32)
    for g in range(R):
        lines = [piece[g * share:(g + 1) * share] for piece in pieces]
        lines = lines + [spare] if spare.shape[0] else lines
        mask[g] = jnp.concatenate(lines, axis=0).astype(bf16)
    left = table[...]
    for first in range(0, CH, group):
        real, imag = [
            jnp.swapaxes(echoes[:, q, first:first + group].astype(f32), 0, 1).astype(bf16)
            for q in range(2)
        ]
        planes = []
        for c in range(group):
            right = jnp.concatenate(
                [jnp.concatenate([real[c], imag[c]], axis=1),
                 jnp.concatenate([imag[c], -real[c]], axis=1)], axis=0)
            planes.append(lax.dot_general(
                left, right, (((1,), (1,)), ((), ())), preferred_element_type=f32))
        turned = jnp.swapaxes(jnp.stack(planes), 0, 1)
        spec[:, first:first + group] = turned.astype(bf16)


def steering(look_index):
    sines = -1.0 + (2.0 * look_index.astype(f32) + 1.0) / ANGLES
    channel_ids = jnp.arange(CH).astype(f32)
    phases = jnp.pi * channel_ids[:, None] * sines[None, :]
    return jnp.concatenate([jnp.cos(phases), jnp.sin(phases)], axis=0)


def exchange_kernel(D, R, spec, mask, wide, mine, masks, send_m, recv_m, send_x, recv_x,
                    send_w, recv_w, own):
    N = D * R
    bins = PULSES // D
    share = bins // R
    d, g = lax.axis_index("dop"), lax.axis_index("rng")
    me = g * D + d
    barrier = pltpu.get_barrier_semaphore()

    def where(j):
        t = lax.rem(me + j, N)
        return t, lax.rem(t, D), t // D

    def greet(j, c):
        _, td, tg = where(j)
        pl.semaphore_signal(barrier, inc=1, device_id=(td, tg), device_id_type=MESH)
        return c

    lax.fori_loop(1, N, greet, 0)
    local = [
        pltpu.make_async_copy(mask.at[g], masks.at[g], own.at[0]),
        pltpu.make_async_copy(spec.at[pl.ds(d * bins + g * share, share + 2)], mine.at[me], own.at[1]),
        pltpu.make_async_copy(spec.at[pl.ds(d * bins, bins + 2)], wide.at[d], own.at[2]),
    ]
    for copy in local:
        copy.start()
    pl.semaphore_wait(barrier, N - 1)

    def mask_copy(j):
        tg = lax.rem(g + j, R)
        return pltpu.make_async_remote_copy(
            mask.at[tg], masks.at[g], send_m.at[j], recv_m.at[g], device_id=(d, tg),
            device_id_type=MESH)

    def mine_copy(j):
        _, td, tg = where(j)
        return pltpu.make_async_remote_copy(
            spec.at[pl.ds(td * bins + tg * share, share + 2)], mine.at[me], send_x.at[j],
            recv_x.at[me], device_id=(td, tg), device_id_type=MESH)

    def wide_copy(j):
        td = lax.rem(d + j, D)
        return pltpu.make_async_remote_copy(
            spec.at[pl.ds(td * bins, bins + 2)], wide.at[d], send_w.at[j], recv_w.at[d],
            device_id=(td, g), device_id_type=MESH)

    def start(make):
        def run(j, c):
            make(j).start()
            return c
        return run

    lax.fori_loop(1, R, start(mask_copy), 0)
    lax.fori_loop(1, N, start(mine_copy), 0)
    lax.fori_loop(1, D, start(wide_copy), 0)

    def end_mask(j, c):
        src = lax.rem(g + j, R)
        mask_copy(j).wait_send()
        pltpu.make_async_remote_copy(
            mask.at[0], masks.at[src], send_m.at[j], recv_m.at[src], device_id=(d, src),
            device_id_type=MESH).wait_recv()
        return c

    def end_mine(j, c):
        src, sd, sg = where(j)
        mine_copy(j).wait_send()
        pltpu.make_async_remote_copy(
            spec.at[pl.ds(0, share + 2)], mine.at[src], send_x.at[j], recv_x.at[src],
            device_id=(sd, sg), device_id_type=MESH).wait_recv()
        return c

    def end_wide(j, c):
        src = lax.rem(d + j, D)
        wide_copy(j).wait_send()
        pltpu.make_async_remote_copy(
            spec.at[pl.ds(0, bins + 2)], wide.at[src], send_w.at[j], recv_w.at[src],
            device_id=(src, g), device_id_type=MESH).wait_recv()
        return c

    lax.fori_loop(1, R, end_mask, 0)
    lax.fori_loop(1, N, end_mine, 0)
    lax.fori_loop(1, D, end_wide, 0)
    for copy in local:
        copy.wait()


def gather_kernel(R, share, unit, out, send, recv, cross_send, cross_recv, hand_send,
                  hand_recv, own):
    H = R // 2
    d, g = lax.axis_index("dop"), lax.axis_index("rng")
    half = g // H * H
    partner = lax.rem(g + H, R)
    other = H - half
    barrier = pltpu.get_barrier_semaphore()

    def peer(j):
        return half + lax.rem(g - half + j, H)

    def greet(j, c):
        pl.semaphore_signal(barrier, inc=1, device_id=(d, peer(j)), device_id_type=MESH)
        return c

    lax.fori_loop(1, H, greet, 0)
    pl.semaphore_signal(barrier, inc=1, device_id=(d, partner), device_id_type=MESH)
    local = [
        pltpu.make_async_copy(unit, out.at[g], own),
    ]
    for copy in local:
        copy.start()
    pl.semaphore_wait(barrier, H)

    def cross(b):
        return pltpu.make_async_remote_copy(
            unit.at[b], out.at[g, b], cross_send.at[b], cross_recv.at[b], device_id=(d, partner),
            device_id_type=MESH)

    def make(j):
        return pltpu.make_async_remote_copy(
            unit, out.at[g], send.at[j], recv.at[g], device_id=(d, peer(j)), device_id_type=MESH)

    def hand(j, b):
        return pltpu.make_async_remote_copy(
            out.at[partner, b], out.at[partner, b], hand_send.at[j, b], hand_recv.at[partner, b],
            device_id=(d, peer(j)), device_id_type=MESH)

    def begin(j, c):
        make(j).start()
        return c

    def end(j, c):
        make(j).wait_send()
        src = peer(j)
        pltpu.make_async_remote_copy(
            unit, out.at[src], send.at[j], recv.at[src], device_id=(d, src),
            device_id_type=MESH).wait_recv()
        far = other + lax.rem(g - half + j, H)
        for b in range(share):
            hand(j, b).wait_send()
            pltpu.make_async_remote_copy(
                unit.at[b], out.at[far, b], hand_send.at[j, b], hand_recv.at[far, b],
                device_id=(d, src), device_id_type=MESH).wait_recv()
        return c

    for b in range(share):
        cross(b).start()
    lax.fori_loop(1, H, begin, 0)
    for b in range(share):
        pltpu.make_async_remote_copy(
            unit.at[b], out.at[partner, b], cross_send.at[b], cross_recv.at[b],
            device_id=(d, partner), device_id_type=MESH).wait_recv()

        def begin_hand(j, c):
            hand(j, b).start()
            return c

        lax.fori_loop(1, H, begin_hand, 0)
    lax.fori_loop(1, H, end, 0)
    for b in range(share):
        cross(b).wait_send()
    for copy in local:
        copy.wait()


def invert(re, im):
    width = re.shape[1]
    lane = lax.broadcasted_iota(jnp.int32, (CH, width), 1)
    row = lax.broadcasted_iota(jnp.int32, (CH, width), 0)
    base = lane // CH * CH
    col = lane - base
    for k in range(CH):
        pick = base + k
        cr = jnp.take_along_axis(re, pick, axis=1)
        ci = jnp.take_along_axis(im, pick, axis=1)
        at_col, at_row = col == k, row == k
        scale = 1.0 / cr[k:k + 1]
        rr = jnp.where(at_col[:1], 1.0, re[k:k + 1]) * scale
        ri = jnp.where(at_col[:1], 0.0, im[k:k + 1]) * scale
        clear = jnp.logical_or(at_col, at_row)
        cr = jnp.where(at_row, -1.0, cr)
        ci = jnp.where(at_row, 0.0, ci)
        re = jnp.where(clear, 0.0, re) - (cr * rr - ci * ri)
        im = jnp.where(clear, 0.0, im) - (cr * ri + ci * rr)
    return re, im


def stacked_form(re, im):
    return jnp.concatenate([re, im], axis=0)


def full_form(stacked):
    re, im = stacked[:CH], stacked[CH:]
    return jnp.concatenate(
        [jnp.concatenate([re, -im], axis=1), jnp.concatenate([im, re], axis=1)], axis=0)


def mul(a, b):
    return jnp.dot(a, b, precision=highest, preferred_element_type=f32)


def invert_all(blocks):
    lanes = 128 // CH
    packed = (blocks * lanes)[:lanes] if len(blocks) < lanes else blocks
    re, im = invert(
        jnp.concatenate([block[:CH] for block in packed], axis=1),
        jnp.concatenate([block[CH:] for block in packed], axis=1))
    return [
        stacked_form(re[:, i * CH:(i + 1) * CH], im[:, i * CH:(i + 1) * CH])
        for i in range(len(blocks))
    ]


def weights_kernel(D, R, share, mine, masks, steer, unit, gram):
    lane = lax.broadcasted_iota(jnp.int32, (CH, 128), 1)
    sign = jnp.where(lane < 64, -1.0, 1.0).astype(bf16)
    gram[...] = jnp.zeros_like(gram)

    def add(g, c):
        rows = masks[g].astype(f32)
        plain = [[mine[g * D + s, b] for s in range(D)] for b in range(share + 2)]
        turned = [[pltpu.roll(x.astype(f32), 64, 1).astype(bf16) * sign for x in line] for line in plain]
        plain_k = [jnp.concatenate(line, axis=1) for line in plain]
        turned_k = [jnp.concatenate(line, axis=1) for line in turned]
        for b in range(share):
            weight = jnp.concatenate(
                [jnp.broadcast_to(rows[s * share + b:s * share + b + 1], (CH, 128)).astype(bf16)
                 for s in range(D)], axis=1)
            left = jnp.concatenate([plain_k[b + i] * weight for i in range(3)], axis=0)
            right = jnp.concatenate(
                [plain_k[b + i] for i in range(3)] + [turned_k[b + i] for i in range(3)], axis=0)
            gram[b] += lax.dot_general(
                left, right, (((1,), (1,)), ((), ())), preferred_element_type=f32)
        return c

    lax.fori_loop(0, R, add, 0)

    eye_r = lax.broadcasted_iota(jnp.int32, (3 * CH, 6 * CH), 0)
    eye_c = lax.broadcasted_iota(jnp.int32, (3 * CH, 6 * CH), 1)
    diagonal = eye_r == eye_c
    cov = []
    for b in range(share):
        whole = gram[b]
        trace = jnp.sum(jnp.where(diagonal, whole, 0.0), keepdims=True)
        power = trace / (3 * CH) + epsilon
        whole = whole / power + jnp.where(diagonal, loading, 0.0)
        cov.append([[
            stacked_form(whole[i * CH:(i + 1) * CH, j * CH:(j + 1) * CH],
                         whole[i * CH:(i + 1) * CH, (3 + j) * CH:(4 + j) * CH])
            for j in range(3)] for i in range(3)])
    every = range(share)
    inverse0 = invert_all([cov[b][0][0] for b in every])
    ahead = [mul(full_form(inverse0[b]), jnp.concatenate([cov[b][0][1], cov[b][0][2]], axis=1))
             for b in every]
    down = [mul(jnp.concatenate([full_form(cov[b][1][0]), full_form(cov[b][2][0])], axis=0), ahead[b])
            for b in every]
    c11 = [cov[b][1][1] - down[b][:2 * CH, :CH] for b in every]
    c12 = [cov[b][1][2] - down[b][:2 * CH, CH:] for b in every]
    c21 = [cov[b][2][1] - down[b][2 * CH:, :CH] for b in every]
    inverse2 = invert_all([cov[b][2][2] - down[b][2 * CH:, CH:] for b in every])
    back = [mul(full_form(inverse2[b]), c21[b]) for b in every]
    inverse1 = invert_all([c11[b] - mul(full_form(c12[b]), back[b]) for b in every])
    steer_here = steer[...]
    for b in every:
        x1 = mul(full_form(inverse1[b]), steer_here)
        x2 = -mul(full_form(back[b]), x1)
        x0 = -(mul(full_form(ahead[b][:, :CH]), x1) + mul(full_form(ahead[b][:, CH:]), x2))
        gain = jnp.sum(steer_here * x1, axis=0, keepdims=True)
        scale = 1.0 / jnp.sqrt(gain)
        parts = [x * scale for x in (x0, x1, x2)]
        unit[b] = jnp.concatenate(
            [jnp.concatenate([x[:CH], x[CH:]], axis=1) for x in parts], axis=0).astype(bf16)


def beams_kernel(D, step_bins, wide, unit, out):
    first = pl.program_id(0) * step_bins
    lane = lax.broadcasted_iota(jnp.int32, (CH, 128), 1)
    sign = jnp.where(lane < 64, 1.0, -1.0).astype(bf16)
    rows = []
    for b in range(step_bins + 2):
        pieces = [wide[s, first + b] for s in range(D)]
        rows.append(jnp.concatenate([x[:, :64] for x in pieces], axis=1))
        rows.append(jnp.concatenate([x[:, 64:] for x in pieces], axis=1))
    for b in range(step_bins):
        weight = []
        for i in range(3):
            u = unit[b, i * CH:(i + 1) * CH]
            weight.append(u * sign)
            weight.append(pltpu.roll(u.astype(f32), 64, 1).astype(bf16))
        out[b] = lax.dot_general(
            jnp.concatenate(weight, axis=0), jnp.concatenate(rows[2 * b:2 * b + 6], axis=0),
            (((0,), (0,)), ((), ())), preferred_element_type=f32)


def body(echoes, training, look_index):
    D, R = lax.axis_size("dop"), lax.axis_size("rng")
    N = D * R
    bins = PULSES // D
    share = bins // R
    cells = echoes.shape[0]
    rows = PULSES + 8
    steer = steering(look_index)
    anywhere = pl.BlockSpec(memory_space=pl.ANY)
    in_vmem = pl.BlockSpec(memory_space=pltpu.VMEM)
    dma = pltpu.SemaphoreType.DMA
    spec, mask = pl.pallas_call(
        functools.partial(spectra_kernel, 16, D, R),
        out_shape=[
            jax.ShapeDtypeStruct((rows, CH, 2 * cells), bf16),
            jax.ShapeDtypeStruct((R, share * D + -share * D % 16, 2 * cells), bf16),
        ],
        in_specs=[in_vmem] * 3,
        out_specs=[in_vmem] * 2,
        compiler_params=pltpu.CompilerParams(vmem_limit_bytes=32 * 1024 * 1024),
        name="spectra",
    )(echoes, twiddle_table(rows), training)
    wide, mine, masks = pl.pallas_call(
        functools.partial(exchange_kernel, D, R),
        out_shape=[
            jax.ShapeDtypeStruct((D, bins + 2, CH, 2 * cells), bf16),
            jax.ShapeDtypeStruct((N, share + 2, CH, 2 * cells), bf16),
            jax.ShapeDtypeStruct(mask.shape, bf16),
        ],
        in_specs=[anywhere] * 2,
        out_specs=[anywhere] * 3,
        scratch_shapes=[dma((R,)), dma((R,)), dma((N,)), dma((N,)), dma((D,)), dma((D,)), dma((3,))],
        compiler_params=pltpu.CompilerParams(collective_id=0, has_side_effects=True),
        name="exchange",
    )(spec, mask)
    unit = pl.pallas_call(
        functools.partial(weights_kernel, D, R, share),
        out_shape=jax.ShapeDtypeStruct((share, 3 * CH, 2 * LOOKS), bf16),
        in_specs=[in_vmem] * 3,
        out_specs=in_vmem,
        scratch_shapes=[pltpu.VMEM((share, 3 * CH, 6 * CH), f32)],
        compiler_params=pltpu.CompilerParams(vmem_limit_bytes=32 * 1024 * 1024),
        name="weights",
    )(mine, masks, steer)
    units = pl.pallas_call(
        functools.partial(gather_kernel, R, share),
        out_shape=jax.ShapeDtypeStruct((R,) + unit.shape, bf16),
        in_specs=[anywhere],
        out_specs=anywhere,
        scratch_shapes=[
            dma((R,)), dma((R,)), dma((share,)), dma((share,)), dma((R, share)), dma((R, share)), dma,
        ],
        compiler_params=pltpu.CompilerParams(collective_id=1, has_side_effects=True),
        name="gather",
    )(unit)
    units = units.reshape(bins, 3 * CH, 2 * LOOKS)
    step_bins = 4
    out = pl.pallas_call(
        functools.partial(beams_kernel, D, step_bins),
        grid=(bins // step_bins,),
        out_shape=jax.ShapeDtypeStruct((bins, 2 * LOOKS, D * cells), f32),
        in_specs=[
            in_vmem,
            pl.BlockSpec((step_bins, 3 * CH, 2 * LOOKS), lambda i: (i, 0, 0)),
        ],
        out_specs=pl.BlockSpec((step_bins, 2 * LOOKS, D * cells), lambda i: (i, 0, 0)),
        compiler_params=pltpu.CompilerParams(vmem_limit_bytes=32 * 1024 * 1024),
        name="beams",
    )(wide, units)
    return out.reshape(bins, 2, LOOKS, D * cells)


def solution(mesh):
    in_specs = (P(("rng", "dop"), None, None, None), P("dop", "rng"), P())
    out_specs = P("dop", None, None, "rng")
    return jax.shard_map(body, mesh=mesh, in_specs=in_specs, out_specs=out_specs, check_vma=False)
```

```python
import functools

import jax
import jax.numpy as jnp
import numpy as np
from jax import lax
from jax.experimental import pallas as pl
from jax.experimental.pallas import tpu as pltpu
from jax.sharding import PartitionSpec as P

CH = 32
PULSES = 128
LOOKS = 64
ANGLES = 256

loading = 0.1
epsilon = 1e-06
highest = lax.Precision.HIGHEST
MESH = pl.DeviceIdType.MESH
bf16 = jnp.bfloat16
f32 = jnp.float32


def twiddle_table(rows):
    pulse_ids = np.arange(PULSES)
    bins = np.arange(-1, rows - 1) % PULSES
    angles = ((bins[:, None] * pulse_ids[None, :]) % PULSES).astype(np.float32) * np.float32(
        2.0 * np.pi / PULSES
    )
    return jnp.asarray(np.concatenate([np.cos(angles), np.sin(angles)], axis=1), bf16)


def spectra_kernel(group, D, R, echoes, table, training, spec, mask):
    cells = echoes.shape[0]
    share = training.shape[0] // R
    trains = training[...].astype(f32)
    pieces = [trains[:, s * cells:(s + 1) * cells] for s in range(D)]
    pieces = [jnp.concatenate([piece, piece], axis=1) for piece in pieces]
    spare = jnp.zeros((-share * D % 16, 2 * cells), f32)
    for g in range(R):
        lines = [piece[g * share:(g + 1) * share] for piece in pieces]
        lines = lines + [spare] if spare.shape[0] else lines
        mask[g] = jnp.concatenate(lines, axis=0).astype(bf16)
    left = table[...]
    for first in range(0, CH, group):
        real, imag = [
            jnp.swapaxes(echoes[:, q, first:first + group].astype(f32), 0, 1).astype(bf16)
            for q in range(2)
        ]
        planes = []
        for c in range(group):
            right = jnp.concatenate(
                [jnp.concatenate([real[c], imag[c]], axis=1),
                 jnp.concatenate([imag[c], -real[c]], axis=1)], axis=0)
            planes.append(lax.dot_general(
                left, right, (((1,), (1,)), ((), ())), preferred_element_type=f32))
        turned = jnp.swapaxes(jnp.stack(planes), 0, 1)
        spec[:, first:first + group] = turned.astype(bf16)


def steering(look_index):
    sines = -1.0 + (2.0 * look_index.astype(f32) + 1.0) / ANGLES
    channel_ids = jnp.arange(CH).astype(f32)
    phases = jnp.pi * channel_ids[:, None] * sines[None, :]
    return jnp.concatenate([jnp.cos(phases), jnp.sin(phases)], axis=0)


def exchange_kernel(D, R, spec, mask, wide, mine, masks, send_m, recv_m, send_x, recv_x,
                    send_w, recv_w, own):
    N = D * R
    bins = PULSES // D
    share = bins // R
    d, g = lax.axis_index("dop"), lax.axis_index("rng")
    me = g * D + d
    barrier = pltpu.get_barrier_semaphore()

    def where(j):
        t = lax.rem(me + j, N)
        return t, lax.rem(t, D), t // D

    def greet(j, c):
        _, td, tg = where(j)
        pl.semaphore_signal(barrier, inc=1, device_id=(td, tg), device_id_type=MESH)
        return c

    lax.fori_loop(1, N, greet, 0)
    local = [
        pltpu.make_async_copy(mask.at[g], masks.at[g], own.at[0]),
        pltpu.make_async_copy(spec.at[pl.ds(d * bins + g * share, share + 2)], mine.at[me], own.at[1]),
        pltpu.make_async_copy(spec.at[pl.ds(d * bins, bins + 2)], wide.at[d], own.at[2]),
    ]
    for copy in local:
        copy.start()
    pl.semaphore_wait(barrier, N - 1)

    def mask_copy(j):
        tg = lax.rem(g + j, R)
        return pltpu.make_async_remote_copy(
            mask.at[tg], masks.at[g], send_m.at[j], recv_m.at[g], device_id=(d, tg),
            device_id_type=MESH)

    def mine_copy(j):
        _, td, tg = where(j)
        return pltpu.make_async_remote_copy(
            spec.at[pl.ds(td * bins + tg * share, share + 2)], mine.at[me], send_x.at[j],
            recv_x.at[me], device_id=(td, tg), device_id_type=MESH)

    def wide_copy(j):
        td = lax.rem(d + j, D)
        return pltpu.make_async_remote_copy(
            spec.at[pl.ds(td * bins, bins + 2)], wide.at[d], send_w.at[j], recv_w.at[d],
            device_id=(td, g), device_id_type=MESH)

    def start(make):
        def run(j, c):
            make(j).start()
            return c
        return run

    lax.fori_loop(1, R, start(mask_copy), 0)
    lax.fori_loop(1, N, start(mine_copy), 0)
    lax.fori_loop(1, D, start(wide_copy), 0)

    def end_mask(j, c):
        src = lax.rem(g + j, R)
        mask_copy(j).wait_send()
        pltpu.make_async_remote_copy(
            mask.at[0], masks.at[src], send_m.at[j], recv_m.at[src], device_id=(d, src),
            device_id_type=MESH).wait_recv()
        return c

    def end_mine(j, c):
        src, sd, sg = where(j)
        mine_copy(j).wait_send()
        pltpu.make_async_remote_copy(
            spec.at[pl.ds(0, share + 2)], mine.at[src], send_x.at[j], recv_x.at[src],
            device_id=(sd, sg), device_id_type=MESH).wait_recv()
        return c

    def end_wide(j, c):
        src = lax.rem(d + j, D)
        wide_copy(j).wait_send()
        pltpu.make_async_remote_copy(
            spec.at[pl.ds(0, bins + 2)], wide.at[src], send_w.at[j], recv_w.at[src],
            device_id=(src, g), device_id_type=MESH).wait_recv()
        return c

    lax.fori_loop(1, R, end_mask, 0)
    lax.fori_loop(1, N, end_mine, 0)
    lax.fori_loop(1, D, end_wide, 0)
    for copy in local:
        copy.wait()


def gather_kernel(R, unit, out, send, recv, pass_on, own):
    H = R // 2
    d, g = lax.axis_index("dop"), lax.axis_index("rng")
    half = g // H * H
    partner = lax.rem(g + H, R)
    other = H - half
    barrier = pltpu.get_barrier_semaphore()

    def peer(j):
        return half + lax.rem(g - half + j, H)

    def greet(j, c):
        pl.semaphore_signal(barrier, inc=1, device_id=(d, peer(j)), device_id_type=MESH)
        return c

    lax.fori_loop(1, H, greet, 0)
    pl.semaphore_signal(barrier, inc=1, device_id=(d, partner), device_id_type=MESH)
    local = pltpu.make_async_copy(unit, out.at[g], own)
    local.start()
    pl.semaphore_wait(barrier, H)

    cross = pltpu.make_async_remote_copy(
        unit, out.at[g], send.at[0], recv.at[g], device_id=(d, partner), device_id_type=MESH)
    cross.start()

    def make(j):
        return pltpu.make_async_remote_copy(
            unit, out.at[g], send.at[j], recv.at[g], device_id=(d, peer(j)), device_id_type=MESH)

    def hand(j):
        return pltpu.make_async_remote_copy(
            out.at[partner], out.at[partner], pass_on.at[j], recv.at[partner],
            device_id=(d, peer(j)), device_id_type=MESH)

    def arrive(src):
        pltpu.make_async_remote_copy(
            unit, out.at[src], send.at[0], recv.at[src], device_id=(d, partner),
            device_id_type=MESH).wait_recv()

    def begin(j, c):
        make(j).start()
        return c

    def begin_hand(j, c):
        hand(j).start()
        return c

    def end(j, c):
        make(j).wait_send()
        hand(j).wait_send()
        arrive(peer(j))
        arrive(other + lax.rem(g - half + j, H))
        return c

    lax.fori_loop(1, H, begin, 0)
    arrive(partner)
    lax.fori_loop(1, H, begin_hand, 0)
    lax.fori_loop(1, H, end, 0)
    cross.wait_send()
    local.wait()


def invert(re, im):
    width = re.shape[1]
    lane = lax.broadcasted_iota(jnp.int32, (CH, width), 1)
    row = lax.broadcasted_iota(jnp.int32, (CH, width), 0)
    base = lane // CH * CH
    col = lane - base
    for k in range(CH):
        pick = base + k
        cr = jnp.take_along_axis(re, pick, axis=1)
        ci = jnp.take_along_axis(im, pick, axis=1)
        at_col, at_row = col == k, row == k
        scale = 1.0 / cr[k:k + 1]
        rr = jnp.where(at_col[:1], 1.0, re[k:k + 1]) * scale
        ri = jnp.where(at_col[:1], 0.0, im[k:k + 1]) * scale
        clear = jnp.logical_or(at_col, at_row)
        cr = jnp.where(at_row, -1.0, cr)
        ci = jnp.where(at_row, 0.0, ci)
        re = jnp.where(clear, 0.0, re) - (cr * rr - ci * ri)
        im = jnp.where(clear, 0.0, im) - (cr * ri + ci * rr)
    return re, im


def stacked_form(re, im):
    return jnp.concatenate([re, im], axis=0)


def full_form(stacked):
    re, im = stacked[:CH], stacked[CH:]
    return jnp.concatenate(
        [jnp.concatenate([re, -im], axis=1), jnp.concatenate([im, re], axis=1)], axis=0)


def mul(a, b):
    return jnp.dot(a, b, precision=highest, preferred_element_type=f32)


def invert_all(blocks):
    lanes = 128 // CH
    packed = (blocks * lanes)[:lanes] if len(blocks) < lanes else blocks
    re, im = invert(
        jnp.concatenate([block[:CH] for block in packed], axis=1),
        jnp.concatenate([block[CH:] for block in packed], axis=1))
    return [
        stacked_form(re[:, i * CH:(i + 1) * CH], im[:, i * CH:(i + 1) * CH])
        for i in range(len(blocks))
    ]


def weights_kernel(D, R, share, mine, masks, steer, unit, gram):
    lane = lax.broadcasted_iota(jnp.int32, (CH, 128), 1)
    sign = jnp.where(lane < 64, -1.0, 1.0).astype(bf16)
    gram[...] = jnp.zeros_like(gram)

    def add(g, c):
        rows = masks[g].astype(f32)
        plain = [[mine[g * D + s, b] for s in range(D)] for b in range(share + 2)]
        turned = [[pltpu.roll(x.astype(f32), 64, 1).astype(bf16) * sign for x in line] for line in plain]
        plain_k = [jnp.concatenate(line, axis=1) for line in plain]
        turned_k = [jnp.concatenate(line, axis=1) for line in turned]
        for b in range(share):
            weight = jnp.concatenate(
                [jnp.broadcast_to(rows[s * share + b:s * share + b + 1], (CH, 128)).astype(bf16)
                 for s in range(D)], axis=1)
            left = jnp.concatenate([plain_k[b + i] * weight for i in range(3)], axis=0)
            right = jnp.concatenate(
                [plain_k[b + i] for i in range(3)] + [turned_k[b + i] for i in range(3)], axis=0)
            gram[b] += lax.dot_general(
                left, right, (((1,), (1,)), ((), ())), preferred_element_type=f32)
        return c

    lax.fori_loop(0, R, add, 0)

    eye_r = lax.broadcasted_iota(jnp.int32, (3 * CH, 6 * CH), 0)
    eye_c = lax.broadcasted_iota(jnp.int32, (3 * CH, 6 * CH), 1)
    diagonal = eye_r == eye_c
    cov = []
    for b in range(share):
        whole = gram[b]
        trace = jnp.sum(jnp.where(diagonal, whole, 0.0), keepdims=True)
        power = trace / (3 * CH) + epsilon
        whole = whole / power + jnp.where(diagonal, loading, 0.0)
        cov.append([[
            stacked_form(whole[i * CH:(i + 1) * CH, j * CH:(j + 1) * CH],
                         whole[i * CH:(i + 1) * CH, (3 + j) * CH:(4 + j) * CH])
            for j in range(3)] for i in range(3)])
    every = range(share)
    inverse0 = invert_all([cov[b][0][0] for b in every])
    ahead = [mul(full_form(inverse0[b]), jnp.concatenate([cov[b][0][1], cov[b][0][2]], axis=1))
             for b in every]
    down = [mul(jnp.concatenate([full_form(cov[b][1][0]), full_form(cov[b][2][0])], axis=0), ahead[b])
            for b in every]
    c11 = [cov[b][1][1] - down[b][:2 * CH, :CH] for b in every]
    c12 = [cov[b][1][2] - down[b][:2 * CH, CH:] for b in every]
    c21 = [cov[b][2][1] - down[b][2 * CH:, :CH] for b in every]
    inverse2 = invert_all([cov[b][2][2] - down[b][2 * CH:, CH:] for b in every])
    back = [mul(full_form(inverse2[b]), c21[b]) for b in every]
    inverse1 = invert_all([c11[b] - mul(full_form(c12[b]), back[b]) for b in every])
    steer_here = steer[...]
    for b in every:
        x1 = mul(full_form(inverse1[b]), steer_here)
        x2 = -mul(full_form(back[b]), x1)
        x0 = -(mul(full_form(ahead[b][:, :CH]), x1) + mul(full_form(ahead[b][:, CH:]), x2))
        gain = jnp.sum(steer_here * x1, axis=0, keepdims=True)
        scale = 1.0 / jnp.sqrt(gain)
        parts = [x * scale for x in (x0, x1, x2)]
        unit[b] = jnp.concatenate(
            [jnp.concatenate([x[:CH], x[CH:]], axis=1) for x in parts], axis=0).astype(bf16)


def beams_kernel(D, step_bins, wide, unit, out):
    first = pl.program_id(0) * step_bins
    lane = lax.broadcasted_iota(jnp.int32, (CH, 128), 1)
    sign = jnp.where(lane < 64, 1.0, -1.0).astype(bf16)
    rows = []
    for b in range(step_bins + 2):
        pieces = [wide[s, first + b] for s in range(D)]
        rows.append(jnp.concatenate([x[:, :64] for x in pieces], axis=1))
        rows.append(jnp.concatenate([x[:, 64:] for x in pieces], axis=1))
    for b in range(step_bins):
        weight = []
        for i in range(3):
            u = unit[b, i * CH:(i + 1) * CH]
            weight.append(u * sign)
            weight.append(pltpu.roll(u.astype(f32), 64, 1).astype(bf16))
        out[b] = lax.dot_general(
            jnp.concatenate(weight, axis=0), jnp.concatenate(rows[2 * b:2 * b + 6], axis=0),
            (((0,), (0,)), ((), ())), preferred_element_type=f32)


def body(echoes, training, look_index):
    D, R = lax.axis_size("dop"), lax.axis_size("rng")
    N = D * R
    bins = PULSES // D
    share = bins // R
    cells = echoes.shape[0]
    rows = PULSES + 8
    steer = steering(look_index)
    anywhere = pl.BlockSpec(memory_space=pl.ANY)
    in_vmem = pl.BlockSpec(memory_space=pltpu.VMEM)
    dma = pltpu.SemaphoreType.DMA
    spec, mask = pl.pallas_call(
        functools.partial(spectra_kernel, 16, D, R),
        out_shape=[
            jax.ShapeDtypeStruct((rows, CH, 2 * cells), bf16),
            jax.ShapeDtypeStruct((R, share * D + -share * D % 16, 2 * cells), bf16),
        ],
        in_specs=[in_vmem] * 3,
        out_specs=[in_vmem] * 2,
        compiler_params=pltpu.CompilerParams(vmem_limit_bytes=32 * 1024 * 1024),
        name="spectra",
    )(echoes, twiddle_table(rows), training)
    wide, mine, masks = pl.pallas_call(
        functools.partial(exchange_kernel, D, R),
        out_shape=[
            jax.ShapeDtypeStruct((D, bins + 2, CH, 2 * cells), bf16),
            jax.ShapeDtypeStruct((N, share + 2, CH, 2 * cells), bf16),
            jax.ShapeDtypeStruct(mask.shape, bf16),
        ],
        in_specs=[anywhere] * 2,
        out_specs=[anywhere] * 3,
        scratch_shapes=[dma((R,)), dma((R,)), dma((N,)), dma((N,)), dma((D,)), dma((D,)), dma((3,))],
        compiler_params=pltpu.CompilerParams(collective_id=0, has_side_effects=True),
        name="exchange",
    )(spec, mask)
    unit = pl.pallas_call(
        functools.partial(weights_kernel, D, R, share),
        out_shape=jax.ShapeDtypeStruct((share, 3 * CH, 2 * LOOKS), bf16),
        in_specs=[in_vmem] * 3,
        out_specs=in_vmem,
        scratch_shapes=[pltpu.VMEM((share, 3 * CH, 6 * CH), f32)],
        compiler_params=pltpu.CompilerParams(vmem_limit_bytes=32 * 1024 * 1024),
        name="weights",
    )(mine, masks, steer)
    units = pl.pallas_call(
        functools.partial(gather_kernel, R),
        out_shape=jax.ShapeDtypeStruct((R,) + unit.shape, bf16),
        in_specs=[anywhere],
        out_specs=anywhere,
        scratch_shapes=[dma((R,)), dma((R,)), dma((R,)), dma],
        compiler_params=pltpu.CompilerParams(collective_id=1, has_side_effects=True),
        name="gather",
    )(unit)
    units = units.reshape(bins, 3 * CH, 2 * LOOKS)
    step_bins = 4
    out = pl.pallas_call(
        functools.partial(beams_kernel, D, step_bins),
        grid=(bins // step_bins,),
        out_shape=jax.ShapeDtypeStruct((bins, 2 * LOOKS, D * cells), f32),
        in_specs=[
            in_vmem,
            pl.BlockSpec((step_bins, 3 * CH, 2 * LOOKS), lambda i: (i, 0, 0)),
        ],
        out_specs=pl.BlockSpec((step_bins, 2 * LOOKS, D * cells), lambda i: (i, 0, 0)),
        compiler_params=pltpu.CompilerParams(vmem_limit_bytes=32 * 1024 * 1024),
        name="beams",
    )(wide, units)
    return out.reshape(bins, 2, LOOKS, D * cells)


def solution(mesh):
    in_specs = (P(("rng", "dop"), None, None, None), P("dop", "rng"), P())
    out_specs = P("dop", None, None, "rng")
    return jax.shard_map(body, mesh=mesh, in_specs=in_specs, out_specs=out_specs, check_vma=False)
```
